32 devices in a mesh: grid: 8 (over y, x, core), orb: 4 (over z).
Axes of the slice: x: 2, y: 2, z: 4, core: 2. Of those that a mesh axis runs over, the one named last changes fastest.
Arguments:
- psi_in: float32 [128, 48, 8, 128], P('orb', 'grid')
- v_local: float32 [48, 8, 128], P('grid'), may hold values from -3 to 0.5
- proj_index: int32 [24, 4, 128], P('grid'), may hold values from 0 to 6143
- proj_value: float32 [24, 4, 4, 128], P('grid'), may hold values from -1.2 to 1.2
- kb_energy: float32 [32, 4], P('grid'), may hold values from 0.5 to 3
Outputs:
- filtered: float32 [128, 48, 8, 128], P('orb', 'grid')
- gram: float32 [128, 128], P('orb', 'grid')
The draws below stay inside these ranges and needn't reach their ends.
All inputs are finite; a program needn't handle non-finite values.
Results may differ from the reference program's by a relative error of at most 0.00005.
Values sent between devices are 32-bit elements; how exact they have to be, the bound alone decides.
A program may use at most 128 MiB of HBM per device.

```python
import jax
import jax.numpy as jnp
from jax import lax

NX = 128
NY = 8
NORB = 128
PROJ = 4
ATOM_SLOTS = 4
PTS = 128
NZ = 48
CELLS = 6144
PIECES = 24
ATOMS = 32
N_GRID = 8


def draw_psi_in(key, part):
    key_own = jax.random.fold_in(key, 11)
    key_shared = jax.random.fold_in(key, 12)
    key_weight = jax.random.fold_in(key, 13)
    own = jnp.clip(jax.random.normal(key_own, (NORB, NZ, NY, NX), jnp.float32), -5.0, 5.0)
    weight = jax.random.uniform(key_weight, (NORB, 1, 1, 1), jnp.float32, -1.0, 1.0)
    shared = jnp.clip(jax.random.normal(key_shared, (1, NZ, NY, NX), jnp.float32), -5.0, 5.0)
    return own + 0.8 * weight * shared


def with_ends(entries, own_key, low, top_value):
    extent = entries.shape
    place = [jax.random.randint(jax.random.fold_in(own_key, axis), (), 0, extent[axis]) for axis in range(len(extent))]
    entries = entries.at[tuple(place)].set(low)
    longest = extent.index(max(extent))
    place[longest] = (place[longest] + 1) % extent[longest]
    return entries.at[tuple(place)].set(top_value)


def block_levels(stream_key, dims, shards, least, largest):
    def one(dim, blocks):
        heights = jax.random.uniform(jax.random.fold_in(jax.random.fold_in(stream_key, 6), dim), (blocks,), jnp.float32, least / len(shards), largest / len(shards))
        return jnp.repeat(jnp.exp(heights), dims[dim] // blocks).reshape((-1,) + (1,) * (len(dims) - dim - 1))

    gain = one(*shards[0])
    for cut in shards[1:]:
        gain = gain * one(*cut)
    return gain


def centred(rng, extent, width, most, pieces=(), kind=jnp.bfloat16):
    drawn = width * jax.random.normal(rng, extent, jnp.float32)
    if pieces:
        drawn = drawn * block_levels(rng, extent, pieces, -0.22, 0.18)
    return jnp.clip(drawn, -most, most).astype(kind)


def setup_inputs(seed: int = 0) -> dict:
    seeds = jax.random.split(jax.random.key(seed), 6)
    psi_in = draw_psi_in(jax.random.fold_in(seeds[5], 71), 0)
    v_local = jnp.clip(-3.0 + 3.5 * jax.random.uniform(seeds[1], (NZ, NY, NX), jnp.float32) ** block_levels(seeds[1], (NZ, NY, NX), ((0, 8),), -0.2, 0.2), -3.0, 0.5)
    proj_index = with_ends(jax.random.randint(seeds[2], (PIECES, ATOM_SLOTS, PTS), 0, CELLS), jax.random.fold_in(seeds[2], 1), 0, CELLS - 1).astype(jnp.int32)
    proj_value = centred(seeds[3], (PIECES, ATOM_SLOTS, PROJ, PTS), 0.2, 1.2, ((0, 8),), jnp.float32)
    kb_energy = jnp.clip(0.5 + 2.5 * jax.random.uniform(seeds[4], (ATOMS, PROJ), jnp.float32) ** block_levels(seeds[4], (ATOMS, PROJ), ((0, 8),), -0.2, 0.2), 0.5, 3.0)
    return {"psi_in": psi_in, "v_local": v_local, "proj_index": proj_index, "proj_value": proj_value, "kb_energy": kb_energy}


LAP_COEF = (-5369.0 / 1800.0, 12.0 / 7.0, -15.0 / 56.0, 10.0 / 189.0, -1.0 / 112.0, 2.0 / 1925.0, -1.0 / 16632.0)
HIGH = lax.Precision.HIGHEST


def laplace_full(field):
    result = 3.0 * LAP_COEF[0] * field
    for axis in (1, 2, 3):
        for offset in range(1, 7):
            result = result + LAP_COEF[offset] * (jnp.roll(field, offset, axis) + jnp.roll(field, -offset, axis))
    return result


def nonlocal_full(field, proj_index, proj_value, kb_energy):
    orbitals = field.shape[0]
    flattened = field.reshape(orbitals, -1)
    global_index = (jnp.arange(N_GRID, dtype=jnp.int32) * CELLS)[:, None, None, None] + proj_index.reshape(N_GRID, 3, ATOM_SLOTS, PTS).astype(jnp.int32)
    columns = global_index.reshape(-1)
    values = proj_value.reshape(N_GRID, 3, ATOM_SLOTS, PROJ, PTS)
    picked = flattened[:, columns].reshape(orbitals, N_GRID, 3, ATOM_SLOTS, PTS)
    partial_value = jnp.einsum('gkamp,ogkap->gkamo', values, picked, precision=HIGH)
    summed = partial_value[:, 1] + jnp.roll(partial_value[:, 2], 1, 0) + jnp.roll(partial_value[:, 0], -1, 0)
    scaled = summed * kb_energy.reshape(N_GRID, ATOM_SLOTS, PROJ)[..., None]
    returned = jnp.stack([jnp.roll(scaled, 1, 0), scaled, jnp.roll(scaled, -1, 0)], axis=1)
    contrib = jnp.einsum('gkamp,gkamo->ogkap', values, returned, precision=HIGH)
    result = jnp.zeros_like(flattened).at[:, columns].add(contrib.reshape(orbitals, -1))
    return result.reshape(field.shape)


def reference(psi_in, v_local, proj_index, proj_value, kb_energy):
    half_width = 6.0
    centre = 8.0
    sigma = half_width / (-3.0 - centre)
    sigma_two = 1.0 / (2.0 / sigma - sigma)

    def hamilton(field):
        return -0.5 * laplace_full(field) + v_local[None] * field + nonlocal_full(field, proj_index, proj_value, kb_energy)

    def filter_block(block):
        first = (hamilton(block) - centre * block) * (sigma / half_width)
        return (hamilton(first) - centre * first) * (2.0 * sigma_two / half_width) - (sigma * sigma_two) * block

    blocks = psi_in.reshape(NORB // 16, 16, NZ, NY, NX)
    filtered = lax.map(filter_block, blocks).reshape(NORB, NZ, NY, NX)
    flattened = filtered.reshape(NORB, -1)
    gram = jnp.dot(flattened, flattened.T, precision=HIGH, preferred_element_type=jnp.float32) / (NX * NY * NZ)
    return filtered, gram
```

```python
import functools

import jax
import jax.numpy as jnp
from jax import lax
from jax.experimental import pallas as pl
from jax.experimental.pallas import tpu as pltpu
from jax.sharding import PartitionSpec as P

LAP_COEF = (
    -5369.0 / 1800.0,
    12.0 / 7.0,
    -15.0 / 56.0,
    10.0 / 189.0,
    -1.0 / 112.0,
    2.0 / 1925.0,
    -1.0 / 16632.0,
)
HALF_WIDTH = 6.0
CENTRE = 8.0
SIGMA = HALF_WIDTH / (-3.0 - CENTRE)
SIGMA_TWO = 1.0 / (2.0 / SIGMA - SIGMA)
MESH = pl.DeviceIdType.MESH
OB = 8
KP = 64
PAIR_PARTNERS = (-2, -1, 1, 2)
F32 = jnp.float32
BF16 = jnp.bfloat16
NT = (((1,), (1,)), ((), ()))


def split(x):
    high = x.astype(BF16).astype(F32)
    return high, x - high


def kernel(
    n_grid, n_orb, ny, planes, chunks,
    psi_ref, v_ref, idx_ref, val_ref, kb_ref,
    out_ref, gram_ref,
    ext, pf, pt, fbuf, abuf, ah, gbuf, grecv, sbuf, srecv, pay, prec,
    h_send, h_recv, p_send, p_recv, a_send, a_recv, g_send, g_recv, s_send, s_recv,
):
    rows = ny * planes
    quarter = rows // n_orb
    lanes = 128
    g = lax.axis_index("grid")
    o = lax.axis_index("orb")

    def grid_id(d):
        return lax.rem(g + d + n_grid, n_grid)

    def orb_id(d):
        return lax.rem(o + d, n_orb)

    barrier = pltpu.get_barrier_semaphore()

    @pl.loop(1, n_grid)
    def _(d):
        pl.semaphore_signal(barrier, inc=1, device_id=(grid_id(d), o), device_id_type=MESH)

    for d in range(1, n_orb):
        pl.semaphore_signal(barrier, inc=1, device_id=(g, orb_id(d)), device_id_type=MESH)

    @pl.loop(0, chunks)
    def _(c):
        @pl.loop(0, rows, unroll=8)
        def _(r):
            ext[0, c, rows + r] = psi_ref[pl.ds(c * OB * rows + r, OB, stride=rows), :]

    pl.semaphore_wait(barrier, n_grid - 1 + n_orb - 1)

    def halo(stage, c, side):
        return pltpu.make_async_remote_copy(
            src_ref=ext.at[stage, c, pl.ds(rows, rows)],
            dst_ref=ext.at[stage, c, pl.ds(0 if side == 0 else 2 * rows, rows)],
            send_sem=h_send.at[stage, c, side],
            recv_sem=h_recv.at[stage, c, side],
            device_id=(grid_id(1 if side == 0 else -1), o),
            device_id_type=MESH,
        )

    def partial_copy(stage, c, i):
        return pltpu.make_async_remote_copy(
            src_ref=pay.at[stage, c],
            dst_ref=prec.at[stage, c, i],
            send_sem=p_send.at[stage, c, i],
            recv_sem=p_recv.at[stage, c, i],
            device_id=(grid_id(PAIR_PARTNERS[i]), o),
            device_id_type=MESH,
        )

    @pl.loop(0, chunks)
    def _(c):
        halo(0, c, 0).start()
        halo(0, c, 1).start()

    pf[:, 48:KP, :] = jnp.zeros((rows, KP - 48, lanes), F32)

    @pl.loop(0, 6)
    def _(q):
        value = val_ref[q]
        upper = lax.broadcasted_iota(jnp.int32, (8, lanes), 0) < 4
        value = jnp.concatenate(
            [jnp.where(upper, value, 0.0), jnp.where(upper, 0.0, value)], axis=1
        )
        index = idx_ref[q]
        high = jnp.broadcast_to(index >> 7, (8, 2 * lanes))
        low = jnp.broadcast_to(index & 127, (lanes, 2 * lanes))
        hot = jnp.where(
            lax.broadcasted_iota(jnp.int32, (lanes, 2 * lanes), 0) == low, 1.0, 0.0
        ).astype(BF16)
        vh, vl = split(value)
        left = jnp.concatenate(
            [jnp.where(high == h, vh, 0.0) for h in range(rows)], axis=0
        ).astype(BF16)
        dense = lax.dot_general(left, hot, NT, preferred_element_type=F32)
        left = jnp.concatenate(
            [jnp.where(high == h, vl, 0.0) for h in range(rows)], axis=0
        ).astype(BF16)
        dense = dense + lax.dot_general(left, hot, NT, preferred_element_type=F32)
        pf[:, pl.ds(pl.multiple_of(q * 8, 8), 8), :] = dense.reshape(rows, 8, lanes)

    @pl.loop(0, rows // 2, unroll=2)
    def _(h):
        both = jnp.concatenate([pf[2 * h], pf[2 * h + 1]], axis=1)
        high, low = split(both)
        pt[h] = jnp.concatenate([high, low], axis=0).astype(BF16)

    lane = lax.broadcasted_iota(jnp.int32, (OB, lanes), 1)

    def project(stage, c):
        def step(h, acc):
            both = jnp.concatenate(
                [ext[stage, c, rows + 2 * h], ext[stage, c, rows + 2 * h + 1]], axis=1
            )
            high, low = split(both)
            left = jnp.concatenate([high, low], axis=0).astype(BF16)
            return acc + lax.dot_general(left, pt[h], NT, preferred_element_type=F32)

        acc = lax.fori_loop(0, rows // 2, step, jnp.zeros((2 * OB, lanes), F32), unroll=4)
        total = acc[:OB] + acc[OB:] + pltpu.roll(acc[:OB], 64, 1)
        pay[stage, c] = jnp.where(lane < 48, total, kb_ref[...])
        for i in range(4):
            partial_copy(stage, c, i).start()

    @pl.loop(0, chunks)
    def _(c):
        project(0, c)

    def returned(stage, c):
        for i in range(4):
            partial_copy(stage, c, i).wait_recv()
        above2, above1, below1, below2 = (prec[stage, c, i] for i in range(4))
        own = pay[stage, c]
        total = (
            own
            + jnp.where(lane < 32, pltpu.roll(below1, 112, 1), 0.0)
            + jnp.where(lane >= 16, pltpu.roll(above1, 16, 1), 0.0)
            + jnp.where(lane < 16, pltpu.roll(below2, 96, 1), 0.0)
            + jnp.where(lane >= 32, pltpu.roll(above2, 32, 1), 0.0)
        )
        energy = jnp.where(
            lane < 16,
            pltpu.roll(below1, 64, 1),
            jnp.where(lane < 32, pltpu.roll(own, 80, 1), pltpu.roll(above1, 96, 1)),
        )
        total = jnp.where(lane < 48, total * energy, 0.0)
        high, low = split(total)
        return jnp.concatenate([high + pltpu.roll(high, 64, 1), low], axis=0).astype(BF16)

    weight_y = [0.0] * ny
    for k in range(1, 7):
        weight_y[k % ny] += LAP_COEF[k]
        weight_y[-k % ny] += LAP_COEF[k]

    def hamilton(stage, c, scale, put):
        coeff = returned(stage, c)
        halo(stage, c, 0).wait_recv()
        halo(stage, c, 1).wait_recv()

        @pl.loop(0, planes)
        def _(z):
            base = rows + z * ny
            centre = [ext[stage, c, base + y] for y in range(ny)]
            v = v_ref[pl.ds(pl.multiple_of(z * ny, ny), ny), :]
            for pair in range(ny // 2):
                part = jnp.dot(
                    coeff, pt[z * (ny // 2) + pair], preferred_element_type=F32
                )
                part = part[:OB] + part[OB:]
                for half in range(2):
                    y = 2 * pair + half
                    f = centre[y]
                    acc = part[:, half * lanes : (half + 1) * lanes]
                    own = v[y : y + 1, :] + (
                        -1.5 * LAP_COEF[0] - CENTRE - 0.5 * weight_y[0]
                    )
                    acc = acc + own * f
                    for k in range(1, 7):
                        both = (
                            ext[stage, c, base + y + ny * k]
                            + ext[stage, c, base + y - ny * k]
                            + pltpu.roll(f, k, 1)
                            + pltpu.roll(f, lanes - k, 1)
                        )
                        acc = acc + (-0.5 * LAP_COEF[k]) * both
                    for k in range(1, ny // 2):
                        acc = acc + (-0.5 * weight_y[k]) * (
                            centre[(y + k) % ny] + centre[(y - k) % ny]
                        )
                    acc = acc + (-0.5 * weight_y[ny // 2]) * centre[(y + ny // 2) % ny]
                    put(z * ny + y, scale * acc)

    @pl.loop(0, chunks)
    def _(c):
        def put(r, value):
            ext[1, c, rows + r] = value

        hamilton(0, c, SIGMA / HALF_WIDTH, put)
        halo(1, c, 0).start()
        halo(1, c, 1).start()
        project(1, c)

    def quarter_copy(c, d):
        other = orb_id(d)
        return pltpu.make_async_remote_copy(
            src_ref=fbuf.at[c, pl.ds(other * quarter, quarter)],
            dst_ref=abuf.at[n_orb - d, c],
            send_sem=a_send.at[c, d],
            recv_sem=a_recv.at[c, n_orb - d],
            device_id=(g, other),
            device_id_type=MESH,
        )

    def quarter_arrival(c, d):
        return pltpu.make_async_remote_copy(
            src_ref=fbuf.at[c, pl.ds(0, quarter)],
            dst_ref=abuf.at[d, c],
            send_sem=a_send.at[c, d],
            recv_sem=a_recv.at[c, d],
            device_id=(g, orb_id(d)),
            device_id_type=MESH,
        )

    @pl.loop(0, chunks)
    def _(c):
        def put(r, value):
            value = value + (-SIGMA * SIGMA_TWO) * ext[0, c, rows + r]
            fbuf[c, r] = value
            out_ref[pl.ds(c * OB * rows + r, OB, stride=rows), :] = value

        hamilton(1, c, 2.0 * SIGMA_TWO / HALF_WIDTH, put)
        for d in range(1, n_orb):
            quarter_copy(c, d).start()
        abuf[0, c] = fbuf[c, pl.ds(o * quarter, quarter)]

    for d in range(1, n_orb):
        @pl.loop(0, chunks)
        def _(c):
            quarter_arrival(c, d).wait_recv()

    per = chunks * OB
    norb = n_orb * per

    @pl.loop(0, n_orb)
    def _(b):
        slot = lax.rem(b - o + n_orb, n_orb)
        place = pl.multiple_of(b * per, per)
        for r in range(quarter):
            block = abuf[slot, :, r].reshape(per, lanes)
            high, low = split(block)
            ah[pl.ds(place, per), r * lanes : (r + 1) * lanes] = high.astype(BF16)
            ah[pl.ds(norb + place, per), r * lanes : (r + 1) * lanes] = low.astype(BF16)

    prod = lax.dot_general(ah[0:norb], ah[...], NT, preferred_element_type=F32)
    gbuf[...] = prod[:, :norb] + prod[:, norb:]
    prod = lax.dot_general(ah[norb:], ah[0:norb], NT, preferred_element_type=F32)
    gbuf[...] += prod

    def rows_copy(d):
        other = orb_id(d)
        return pltpu.make_async_remote_copy(
            src_ref=gbuf.at[pl.ds(pl.multiple_of(other * per, per), per)],
            dst_ref=grecv.at[n_orb - d],
            send_sem=g_send.at[d],
            recv_sem=g_recv.at[n_orb - d],
            device_id=(g, other),
            device_id_type=MESH,
        )

    def rows_arrival(d):
        return pltpu.make_async_remote_copy(
            src_ref=gbuf.at[pl.ds(0, per)],
            dst_ref=grecv.at[d],
            send_sem=g_send.at[d],
            recv_sem=g_recv.at[d],
            device_id=(g, orb_id(d)),
            device_id_type=MESH,
        )

    for d in range(1, n_orb):
        rows_copy(d).start()
    total = gbuf[pl.ds(pl.multiple_of(o * per, per), per)]
    for d in range(1, n_orb):
        rows_arrival(d).wait_recv()
        total = total + grecv[d]
    sbuf[...] = total

    def sum_copy(d):
        return pltpu.make_async_remote_copy(
            src_ref=sbuf,
            dst_ref=srecv.at[n_grid - d],
            send_sem=s_send.at[d],
            recv_sem=s_recv.at[n_grid - d],
            device_id=(grid_id(d), o),
            device_id_type=MESH,
        )

    def sum_arrival(d):
        return pltpu.make_async_remote_copy(
            src_ref=sbuf,
            dst_ref=srecv.at[d],
            send_sem=s_send.at[d],
            recv_sem=s_recv.at[d],
            device_id=(grid_id(d), o),
            device_id_type=MESH,
        )

    @pl.loop(1, n_grid)
    def _(d):
        sum_copy(d).start()

    @pl.loop(1, n_grid)
    def _(d):
        sum_arrival(d).wait_recv()

    total = sbuf[...]
    total = lax.fori_loop(1, n_grid, lambda d, acc: acc + srecv[d], total)
    columns = norb // n_grid
    total = pltpu.roll(total, lax.rem(norb - g * columns, norb), 1)
    gram_ref[...] = total[:, :columns] * (1.0 / (n_grid * rows * lanes))

    @pl.loop(0, chunks)
    def _(c):
        for stage in range(2):
            for side in range(2):
                halo(stage, c, side).wait_send()
            for i in range(4):
                partial_copy(stage, c, i).wait_send()
        for d in range(1, n_orb):
            quarter_copy(c, d).wait_send()

    for d in range(1, n_orb):
        rows_copy(d).wait_send()

    @pl.loop(1, n_grid)
    def _(d):
        sum_copy(d).wait_send()


def on_device(psi_in, v_local, proj_index, proj_value, kb_energy):
    n_grid = lax.axis_size("grid")
    n_orb = lax.axis_size("orb")
    orbitals, planes, ny, nx = psi_in.shape
    rows = planes * ny
    chunks = orbitals // OB
    norb = orbitals * n_orb
    quarter = rows // n_orb
    psi = psi_in.reshape(orbitals * rows, nx)
    v = v_local.reshape(rows, nx)
    index = proj_index.reshape(6, 1, 2 * nx)
    value = proj_value.reshape(6, 8, nx)
    kb = jnp.broadcast_to(jnp.pad(kb_energy.reshape(1, 16), ((0, 0), (64, 48))), (OB, nx))
    dma = pltpu.SemaphoreType.DMA
    vmem = pl.BlockSpec(memory_space=pltpu.VMEM)
    filtered, gram = pl.pallas_call(
        functools.partial(kernel, n_grid, n_orb, ny, planes, chunks),
        out_shape=(
            jax.ShapeDtypeStruct((orbitals * rows, nx), F32),
            jax.ShapeDtypeStruct((orbitals, norb // n_grid), F32),
        ),
        in_specs=[vmem] * 5,
        out_specs=(vmem, vmem),
        scratch_shapes=[
            pltpu.VMEM((2, chunks, 3 * rows, OB, nx), F32),
            pltpu.VMEM((rows, KP, nx), F32),
            pltpu.VMEM((rows // 2, 2 * KP, 2 * nx), BF16),
            pltpu.VMEM((chunks, rows, OB, nx), F32),
            pltpu.VMEM((n_orb, chunks, quarter, OB, nx), F32),
            pltpu.VMEM((2 * norb, quarter * nx), BF16),
            pltpu.VMEM((norb, norb), F32),
            pltpu.VMEM((n_orb, orbitals, norb), F32),
            pltpu.VMEM((orbitals, norb), F32),
            pltpu.VMEM((n_grid, orbitals, norb), F32),
            pltpu.VMEM((2, chunks, OB, nx), F32),
            pltpu.VMEM((2, chunks, 4, OB, nx), F32),
            dma((2, chunks, 2)),
            dma((2, chunks, 2)),
            dma((2, chunks, 4)),
            dma((2, chunks, 4)),
            dma((chunks, n_orb)),
            dma((chunks, n_orb)),
            dma((n_orb,)),
            dma((n_orb,)),
            dma((n_grid,)),
            dma((n_grid,)),
        ],
        compiler_params=pltpu.CompilerParams(
            collective_id=0, has_side_effects=True, vmem_limit_bytes=40 * 1024 * 1024
        ),
        cost_estimate=pl.CostEstimate(
            flops=400_000_000, bytes_accessed=2_000_000, transcendentals=0
        ),
    )(psi, v, index, value, kb)
    return filtered.reshape(psi_in.shape), gram


def solution(mesh):
    placed = (
        P("orb", "grid", None, None),
        P("grid", None, None),
        P("grid", None, None),
        P("grid", None, None, None),
        P("grid", None),
    )
    return jax.shard_map(
        on_device,
        mesh=mesh,
        in_specs=placed,
        out_specs=(P("orb", "grid", None, None), P("orb", "grid")),
        check_vma=False,
    )
```

```python
import functools

import jax
import jax.numpy as jnp
from jax import lax
from jax.experimental import pallas as pl
from jax.experimental.pallas import tpu as pltpu
from jax.sharding import PartitionSpec as P

LAP_COEF = (
    -5369.0 / 1800.0,
    12.0 / 7.0,
    -15.0 / 56.0,
    10.0 / 189.0,
    -1.0 / 112.0,
    2.0 / 1925.0,
    -1.0 / 16632.0,
)
HALF_WIDTH = 6.0
CENTRE = 8.0
SIGMA = HALF_WIDTH / (-3.0 - CENTRE)
SIGMA_TWO = 1.0 / (2.0 / SIGMA - SIGMA)
MESH = pl.DeviceIdType.MESH
OB = 8
KP = 64
PAIR_PARTNERS = (-2, -1, 1, 2)
F32 = jnp.float32
BF16 = jnp.bfloat16
NT = (((1,), (1,)), ((), ()))


def split(x):
    high = x.astype(BF16).astype(F32)
    return high, x - high


def kernel(
    n_grid, n_orb, ny, planes, chunks,
    psi_hbm, v_hbm, idx_hbm, val_hbm, kb_hbm,
    out_ref, gram_ref,
    psi_ref, v_ref, idx_ref, val_ref, kb_ref, con, ext, pf, pt, fbuf, abuf, ah, gbuf, grecv, sbuf, srecv, pay, prec,
    h_send, h_recv, p_send, p_recv, a_send, a_recv, g_send, g_recv, s_send, s_recv, in_sem, psi_sem,
):
    rows = ny * planes
    quarter = rows // n_orb
    lanes = 128
    g = lax.axis_index("grid")
    o = lax.axis_index("orb")

    def grid_id(d):
        return lax.rem(g + d + n_grid, n_grid)

    def orb_id(d):
        return lax.rem(o + d, n_orb)

    def psi_copy(c):
        part = pl.ds(c * OB * rows, OB * rows)
        return pltpu.make_async_copy(psi_hbm.at[part], psi_ref.at[part], psi_sem.at[c])

    small = [
        pltpu.make_async_copy(src, dst, in_sem.at[i])
        for i, (src, dst) in enumerate(
            ((idx_hbm, idx_ref), (val_hbm, val_ref), (kb_hbm, kb_ref), (v_hbm, v_ref))
        )
    ]

    @pl.loop(0, chunks)
    def _(c):
        psi_copy(c).start()

    for copy in small:
        copy.start()

    barrier = pltpu.get_barrier_semaphore()

    @pl.loop(1, n_grid)
    def _(d):
        pl.semaphore_signal(barrier, inc=1, device_id=(grid_id(d), o), device_id_type=MESH)

    for d in range(1, n_orb):
        pl.semaphore_signal(barrier, inc=1, device_id=(g, orb_id(d)), device_id_type=MESH)

    @pl.loop(0, chunks)
    def _(c):
        psi_copy(c).wait()

        @pl.loop(0, rows, unroll=8)
        def _(r):
            ext[0, c, rows + r] = psi_ref[pl.ds(c * OB * rows + r, OB, stride=rows), :]

    for copy in small:
        copy.wait()

    pl.semaphore_wait(barrier, n_grid - 1 + n_orb - 1)

    def halo(stage, c, side):
        return pltpu.make_async_remote_copy(
            src_ref=ext.at[stage, c, pl.ds(rows, rows)],
            dst_ref=ext.at[stage, c, pl.ds(0 if side == 0 else 2 * rows, rows)],
            send_sem=h_send.at[stage, c, side],
            recv_sem=h_recv.at[stage, c, side],
            device_id=(grid_id(1 if side == 0 else -1), o),
            device_id_type=MESH,
        )

    def partial_copy(stage, c, i):
        return pltpu.make_async_remote_copy(
            src_ref=pay.at[stage, c],
            dst_ref=prec.at[stage, c, i],
            send_sem=p_send.at[stage, c, i],
            recv_sem=p_recv.at[stage, c, i],
            device_id=(grid_id(PAIR_PARTNERS[i]), o),
            device_id_type=MESH,
        )

    def halo_start(stage, c):
        halo(stage, c, 0).start()
        halo(stage, c, 1).start()

    def halo_left(stage, c):
        halo(stage, c, 0).wait_send()
        halo(stage, c, 1).wait_send()

    for c in range(2):
        halo_start(0, c)

    pf[:, 48:KP, :] = jnp.zeros((rows, KP - 48, lanes), F32)

    @pl.loop(0, 6)
    def _(q):
        value = val_ref[q]
        upper = lax.broadcasted_iota(jnp.int32, (8, lanes), 0) < 4
        value = jnp.concatenate(
            [jnp.where(upper, value, 0.0), jnp.where(upper, 0.0, value)], axis=1
        )
        index = idx_ref[q]
        high = jnp.broadcast_to(index >> 7, (8, 2 * lanes))
        low = jnp.broadcast_to(index & 127, (lanes, 2 * lanes))
        hot = jnp.where(
            lax.broadcasted_iota(jnp.int32, (lanes, 2 * lanes), 0) == low, 1.0, 0.0
        ).astype(BF16)
        vh, vl = split(value)
        left = jnp.concatenate(
            [jnp.where(high == h, vh, 0.0) for h in range(rows)], axis=0
        ).astype(BF16)
        dense = lax.dot_general(left, hot, NT, preferred_element_type=F32)
        left = jnp.concatenate(
            [jnp.where(high == h, vl, 0.0) for h in range(rows)], axis=0
        ).astype(BF16)
        dense = dense + lax.dot_general(left, hot, NT, preferred_element_type=F32)
        pf[:, pl.ds(pl.multiple_of(q * 8, 8), 8), :] = dense.reshape(rows, 8, lanes)

    @pl.loop(0, rows // 2, unroll=2)
    def _(h):
        both = jnp.concatenate([pf[2 * h], pf[2 * h + 1]], axis=1)
        high, low = split(both)
        pt[h] = jnp.concatenate([high, low], axis=0).astype(BF16)

    lane = lax.broadcasted_iota(jnp.int32, (OB, lanes), 1)

    energies = jnp.zeros((OB, lanes), F32)
    for a in range(4):
        for m in range(4):
            energies = jnp.where(lane == 64 + 4 * a + m, kb_ref[a : a + 1, m : m + 1], energies)

    def project(stage, first, count):
        def step(h, acc):
            both = jnp.concatenate(
                [
                    jnp.concatenate(
                        [ext[stage, first + i, rows + 2 * h + j] for i in range(count)], axis=0
                    )
                    for j in range(2)
                ],
                axis=1,
            )
            high, low = split(both)
            left = jnp.concatenate([high, low], axis=0).astype(BF16)
            return acc + lax.dot_general(left, pt[h], NT, preferred_element_type=F32)

        most = count * OB
        acc = lax.fori_loop(0, rows // 2, step, jnp.zeros((2 * most, lanes), F32), unroll=4)
        total = acc[:most] + acc[most:] + pltpu.roll(acc[:most], 64, 1)
        for i in range(count):
            pay[stage, first + i] = jnp.where(
                lane < 48, total[i * OB : (i + 1) * OB], energies
            )
            for partner in range(4):
                partial_copy(stage, first + i, partner).start()

    halo_left(0, 0)
    halo_start(0, 2)
    project(0, 0, chunks)
    halo_left(0, 1)
    halo_start(0, 3)

    def returned(stage, c):
        for i in range(4):
            partial_copy(stage, c, i).wait_recv()
        above2, above1, below1, below2 = (prec[stage, c, i] for i in range(4))
        own = pay[stage, c]
        total = (
            own
            + jnp.where(lane < 32, pltpu.roll(below1, 112, 1), 0.0)
            + jnp.where(lane >= 16, pltpu.roll(above1, 16, 1), 0.0)
            + jnp.where(lane < 16, pltpu.roll(below2, 96, 1), 0.0)
            + jnp.where(lane >= 32, pltpu.roll(above2, 32, 1), 0.0)
        )
        energy = jnp.where(
            lane < 16,
            pltpu.roll(below1, 64, 1),
            jnp.where(lane < 32, pltpu.roll(own, 80, 1), pltpu.roll(above1, 96, 1)),
        )
        total = jnp.where(lane < 48, total * energy, 0.0)
        high, low = split(total)
        return high + pltpu.roll(high, 64, 1), low

    def contribute(stage, first, count):
        parts = [returned(stage, first + i) for i in range(count)]
        coeff = jnp.concatenate(
            [high for high, _ in parts] + [low for _, low in parts], axis=0
        ).astype(BF16)
        most = count * OB

        @pl.loop(0, rows // 2, unroll=4)
        def _(h):
            part = jnp.dot(coeff, pt[h], preferred_element_type=F32)
            part = part[:most] + part[most:]
            for i in range(count):
                for half in range(2):
                    con[first + i, 2 * h + half] = part[
                        i * OB : (i + 1) * OB, half * lanes : (half + 1) * lanes
                    ]

    weight_y = [0.0] * ny
    for k in range(1, 7):
        weight_y[k % ny] += LAP_COEF[k]
        weight_y[-k % ny] += LAP_COEF[k]

    def hamilton(stage, c, scale, put):
        halo(stage, c, 0).wait_recv()
        halo(stage, c, 1).wait_recv()

        @pl.loop(0, planes)
        def _(z):
            base = rows + z * ny
            centre = [ext[stage, c, base + y] for y in range(ny)]
            v = v_ref[pl.ds(pl.multiple_of(z * ny, ny), ny), :]
            for y in range(ny):
                f = centre[y]
                acc = con[c, z * ny + y]
                own = v[y : y + 1, :] + (
                    -1.5 * LAP_COEF[0] - CENTRE - 0.5 * weight_y[0]
                )
                acc = acc + own * f
                for k in range(1, 7):
                    both = (
                        ext[stage, c, base + y + ny * k]
                        + ext[stage, c, base + y - ny * k]
                        + pltpu.roll(f, k, 1)
                        + pltpu.roll(f, lanes - k, 1)
                    )
                    acc = acc + (-0.5 * LAP_COEF[k]) * both
                for k in range(1, ny // 2):
                    acc = acc + (-0.5 * weight_y[k]) * (
                        centre[(y + k) % ny] + centre[(y - k) % ny]
                    )
                acc = acc + (-0.5 * weight_y[ny // 2]) * centre[(y + ny // 2) % ny]
                put(z * ny + y, scale * acc)

    contribute(0, 0, chunks)

    @pl.loop(0, chunks // 2)
    def _(pair):
        @pl.loop(2 * pair, 2 * pair + 2)
        def _(c):
            def put(r, value):
                ext[1, c, rows + r] = value

            hamilton(0, c, SIGMA / HALF_WIDTH, put)
            halo_start(1, c)

        project(1, 2 * pair, 2)

    def quarter_copy(c, d):
        other = orb_id(d)
        return pltpu.make_async_remote_copy(
            src_ref=fbuf.at[c, pl.ds(other * quarter, quarter)],
            dst_ref=abuf.at[n_orb - d, c],
            send_sem=a_send.at[c, d],
            recv_sem=a_recv.at[c, n_orb - d],
            device_id=(g, other),
            device_id_type=MESH,
        )

    def quarter_arrival(c, d):
        return pltpu.make_async_remote_copy(
            src_ref=fbuf.at[c, pl.ds(0, quarter)],
            dst_ref=abuf.at[d, c],
            send_sem=a_send.at[c, d],
            recv_sem=a_recv.at[c, d],
            device_id=(g, orb_id(d)),
            device_id_type=MESH,
        )

    @pl.loop(0, chunks // 2)
    def _(pair):
        contribute(1, 2 * pair, 2)

        @pl.loop(2 * pair, 2 * pair + 2)
        def _(c):
            def put(r, value):
                value = value + (-SIGMA * SIGMA_TWO) * ext[0, c, rows + r]
                fbuf[c, r] = value
                out_ref[pl.ds(c * OB * rows + r, OB, stride=rows), :] = value

            hamilton(1, c, 2.0 * SIGMA_TWO / HALF_WIDTH, put)
            for d in range(1, n_orb):
                quarter_copy(c, d).start()
            abuf[0, c] = fbuf[c, pl.ds(o * quarter, quarter)]

    for d in range(1, n_orb):
        @pl.loop(0, chunks)
        def _(c):
            quarter_arrival(c, d).wait_recv()

    per = chunks * OB
    norb = n_orb * per

    @pl.loop(0, n_orb)
    def _(b):
        slot = lax.rem(b - o + n_orb, n_orb)
        place = pl.multiple_of(b * per, per)
        for r in range(quarter):
            block = abuf[slot, :, r].reshape(per, lanes)
            high, low = split(block)
            ah[pl.ds(place, per), r * lanes : (r + 1) * lanes] = high.astype(BF16)
            ah[pl.ds(norb + place, per), r * lanes : (r + 1) * lanes] = low.astype(BF16)

    prod = lax.dot_general(ah[0:norb], ah[...], NT, preferred_element_type=F32)
    gbuf[...] = prod[:, :norb] + prod[:, norb:]
    prod = lax.dot_general(ah[norb:], ah[0:norb], NT, preferred_element_type=F32)
    gbuf[...] += prod

    def rows_copy(d):
        other = orb_id(d)
        return pltpu.make_async_remote_copy(
            src_ref=gbuf.at[pl.ds(pl.multiple_of(other * per, per), per)],
            dst_ref=grecv.at[n_orb - d],
            send_sem=g_send.at[d],
            recv_sem=g_recv.at[n_orb - d],
            device_id=(g, other),
            device_id_type=MESH,
        )

    def rows_arrival(d):
        return pltpu.make_async_remote_copy(
            src_ref=gbuf.at[pl.ds(0, per)],
            dst_ref=grecv.at[d],
            send_sem=g_send.at[d],
            recv_sem=g_recv.at[d],
            device_id=(g, orb_id(d)),
            device_id_type=MESH,
        )

    for d in range(1, n_orb):
        rows_copy(d).start()
    total = gbuf[pl.ds(pl.multiple_of(o * per, per), per)]
    for d in range(1, n_orb):
        rows_arrival(d).wait_recv()
        total = total + grecv[d]
    sbuf[...] = total

    def sum_copy(d):
        return pltpu.make_async_remote_copy(
            src_ref=sbuf,
            dst_ref=srecv.at[n_grid - d],
            send_sem=s_send.at[d],
            recv_sem=s_recv.at[n_grid - d],
            device_id=(grid_id(d), o),
            device_id_type=MESH,
        )

    def sum_arrival(d):
        return pltpu.make_async_remote_copy(
            src_ref=sbuf,
            dst_ref=srecv.at[d],
            send_sem=s_send.at[d],
            recv_sem=s_recv.at[d],
            device_id=(grid_id(d), o),
            device_id_type=MESH,
        )

    @pl.loop(1, n_grid)
    def _(d):
        sum_copy(d).start()

    @pl.loop(1, n_grid)
    def _(d):
        sum_arrival(d).wait_recv()

    total = sbuf[...]
    total = lax.fori_loop(1, n_grid, lambda d, acc: acc + srecv[d], total)
    columns = norb // n_grid
    total = pltpu.roll(total, lax.rem(norb - g * columns, norb), 1)
    gram_ref[...] = total.T[:columns] * (1.0 / (n_grid * rows * lanes))

    @pl.loop(0, chunks)
    def _(c):
        halo_left(1, c)
        for stage in range(2):
            for i in range(4):
                partial_copy(stage, c, i).wait_send()
        for d in range(1, n_orb):
            quarter_copy(c, d).wait_send()

    for c in range(2, 4):
        halo_left(0, c)

    for d in range(1, n_orb):
        rows_copy(d).wait_send()

    @pl.loop(1, n_grid)
    def _(d):
        sum_copy(d).wait_send()


def on_device(psi_in, v_local, proj_index, proj_value, kb_energy):
    n_grid = lax.axis_size("grid")
    n_orb = lax.axis_size("orb")
    orbitals, planes, ny, nx = psi_in.shape
    rows = planes * ny
    chunks = orbitals // OB
    norb = orbitals * n_orb
    quarter = rows // n_orb
    psi = psi_in.reshape(orbitals * rows, nx)
    v = v_local.reshape(rows, nx)
    index = proj_index.reshape(6, 1, 2 * nx)
    value = proj_value.reshape(6, 8, nx)
    dma = pltpu.SemaphoreType.DMA
    vmem = pl.BlockSpec(memory_space=pltpu.VMEM)
    hbm = pl.BlockSpec(memory_space=pltpu.HBM)
    filtered, gram = pl.pallas_call(
        functools.partial(kernel, n_grid, n_orb, ny, planes, chunks),
        out_shape=(
            jax.ShapeDtypeStruct((orbitals * rows, nx), F32),
            jax.ShapeDtypeStruct((norb // n_grid, orbitals), F32),
        ),
        in_specs=[hbm] * 5,
        out_specs=(vmem, vmem),
        scratch_shapes=[
            pltpu.VMEM(psi.shape, F32),
            pltpu.VMEM(v.shape, F32),
            pltpu.VMEM(index.shape, jnp.int32),
            pltpu.VMEM(value.shape, F32),
            pltpu.VMEM(kb_energy.shape, F32),
            pltpu.VMEM((chunks, rows, OB, nx), F32),
            pltpu.VMEM((2, chunks, 3 * rows, OB, nx), F32),
            pltpu.VMEM((rows, KP, nx), F32),
            pltpu.VMEM((rows // 2, 2 * KP, 2 * nx), BF16),
            pltpu.VMEM((chunks, rows, OB, nx), F32),
            pltpu.VMEM((n_orb, chunks, quarter, OB, nx), F32),
            pltpu.VMEM((2 * norb, quarter * nx), BF16),
            pltpu.VMEM((norb, norb), F32),
            pltpu.VMEM((n_orb, orbitals, norb), F32),
            pltpu.VMEM((orbitals, norb), F32),
            pltpu.VMEM((n_grid, orbitals, norb), F32),
            pltpu.VMEM((2, chunks, OB, nx), F32),
            pltpu.VMEM((2, chunks, 4, OB, nx), F32),
            dma((2, chunks, 2)),
            dma((2, chunks, 2)),
            dma((2, chunks, 4)),
            dma((2, chunks, 4)),
            dma((chunks, n_orb)),
            dma((chunks, n_orb)),
            dma((n_orb,)),
            dma((n_orb,)),
            dma((n_grid,)),
            dma((n_grid,)),
            dma((4,)),
            dma((chunks,)),
        ],
        compiler_params=pltpu.CompilerParams(
            collective_id=0, has_side_effects=True, vmem_limit_bytes=62 * 1024 * 1024
        ),
        cost_estimate=pl.CostEstimate(
            flops=400_000_000, bytes_accessed=2_000_000, transcendentals=0
        ),
    )(psi, v, index, value, kb_energy)
    return filtered.reshape(psi_in.shape), gram.T


def solution(mesh):
    placed = (
        P("orb", "grid", None, None),
        P("grid", None, None),
        P("grid", None, None),
        P("grid", None, None, None),
        P("grid", None),
    )
    return jax.shard_map(
        on_device,
        mesh=mesh,
        in_specs=placed,
        out_specs=(P("orb", "grid", None, None), P("orb", "grid")),
        check_vma=False,
    )
```

```python
import functools

import jax
import jax.numpy as jnp
from jax import lax
from jax.experimental import pallas as pl
from jax.experimental.pallas import tpu as pltpu
from jax.sharding import PartitionSpec as P

LAP_COEF = (
    -5369.0 / 1800.0,
    12.0 / 7.0,
    -15.0 / 56.0,
    10.0 / 189.0,
    -1.0 / 112.0,
    2.0 / 1925.0,
    -1.0 / 16632.0,
)
HALF_WIDTH = 6.0
CENTRE = 8.0
SIGMA = HALF_WIDTH / (-3.0 - CENTRE)
SIGMA_TWO = 1.0 / (2.0 / SIGMA - SIGMA)
MESH = pl.DeviceIdType.MESH
OB = 8
KP = 64
PAIR_PARTNERS = (-2, -1, 1, 2)
F32 = jnp.float32
BF16 = jnp.bfloat16
NT = (((1,), (1,)), ((), ()))


def split(x):
    high = x.astype(BF16).astype(F32)
    return high, x - high


def kernel(
    n_grid, n_orb, ny, planes, chunks,
    psi_hbm, v_hbm, idx_hbm, val_hbm, kb_hbm,
    out_hbm, gram_ref,
    out_ref,    psi_ref, v_ref, idx_ref, val_ref, kb_ref, con, ext, pf, pt, fbuf, abuf, ah, gbuf, grecv, sbuf, srecv, pay, prec,
    h_send, h_recv, p_send, p_recv, a_send, a_recv, g_send, g_recv, s_send, s_recv, in_sem, psi_sem, out_sem,
):
    rows = ny * planes
    quarter = rows // n_orb
    lanes = 128
    g = lax.axis_index("grid")
    o = lax.axis_index("orb")

    def grid_id(d):
        return lax.rem(g + d + n_grid, n_grid)

    def orb_id(d):
        return lax.rem(o + d, n_orb)

    def psi_copy(c):
        part = pl.ds(c * OB * rows, OB * rows)
        return pltpu.make_async_copy(psi_hbm.at[part], psi_ref.at[part], psi_sem.at[c])

    small = [
        pltpu.make_async_copy(src, dst, in_sem.at[i])
        for i, (src, dst) in enumerate(
            ((idx_hbm, idx_ref), (val_hbm, val_ref), (kb_hbm, kb_ref), (v_hbm, v_ref))
        )
    ]

    @pl.loop(0, chunks)
    def _(c):
        psi_copy(c).start()

    for copy in small:
        copy.start()

    barrier = pltpu.get_barrier_semaphore()

    @pl.loop(1, n_grid)
    def _(d):
        pl.semaphore_signal(barrier, inc=1, device_id=(grid_id(d), o), device_id_type=MESH)

    for d in range(1, n_orb):
        pl.semaphore_signal(barrier, inc=1, device_id=(g, orb_id(d)), device_id_type=MESH)

    @pl.loop(0, chunks)
    def _(c):
        psi_copy(c).wait()

        @pl.loop(0, rows, unroll=8)
        def _(r):
            ext[0, c, rows + r] = psi_ref[pl.ds(c * OB * rows + r, OB, stride=rows), :]

    for copy in small:
        copy.wait()

    pl.semaphore_wait(barrier, n_grid - 1 + n_orb - 1)

    def halo(stage, c, side):
        return pltpu.make_async_remote_copy(
            src_ref=ext.at[stage, c, pl.ds(rows, rows)],
            dst_ref=ext.at[stage, c, pl.ds(0 if side == 0 else 2 * rows, rows)],
            send_sem=h_send.at[stage, c, side],
            recv_sem=h_recv.at[stage, c, side],
            device_id=(grid_id(1 if side == 0 else -1), o),
            device_id_type=MESH,
        )

    def partial_copy(stage, c, i):
        return pltpu.make_async_remote_copy(
            src_ref=pay.at[stage, c],
            dst_ref=prec.at[stage, c, i],
            send_sem=p_send.at[stage, c, i],
            recv_sem=p_recv.at[stage, c, i],
            device_id=(grid_id(PAIR_PARTNERS[i]), o),
            device_id_type=MESH,
        )

    def halo_start(stage, c):
        halo(stage, c, 0).start()
        halo(stage, c, 1).start()

    def halo_left(stage, c):
        halo(stage, c, 0).wait_send()
        halo(stage, c, 1).wait_send()

    def advance(k):
        halo_left((k - 1) // chunks, (k - 1) % chunks)
        halo_start(k // chunks, k % chunks)

    halo_start(0, 0)

    pf[:, 48:KP, :] = jnp.zeros((rows, KP - 48, lanes), F32)

    @pl.loop(0, 6)
    def _(q):
        value = val_ref[q]
        upper = lax.broadcasted_iota(jnp.int32, (8, lanes), 0) < 4
        value = jnp.concatenate(
            [jnp.where(upper, value, 0.0), jnp.where(upper, 0.0, value)], axis=1
        )
        index = idx_ref[q]
        high = jnp.broadcast_to(index >> 7, (8, 2 * lanes))
        low = jnp.broadcast_to(index & 127, (lanes, 2 * lanes))
        hot = jnp.where(
            lax.broadcasted_iota(jnp.int32, (lanes, 2 * lanes), 0) == low, 1.0, 0.0
        ).astype(BF16)
        vh, vl = split(value)
        left = jnp.concatenate(
            [jnp.where(high == h, vh, 0.0) for h in range(rows)], axis=0
        ).astype(BF16)
        dense = lax.dot_general(left, hot, NT, preferred_element_type=F32)
        left = jnp.concatenate(
            [jnp.where(high == h, vl, 0.0) for h in range(rows)], axis=0
        ).astype(BF16)
        dense = dense + lax.dot_general(left, hot, NT, preferred_element_type=F32)
        pf[:, pl.ds(pl.multiple_of(q * 8, 8), 8), :] = dense.reshape(rows, 8, lanes)

    advance(1)

    @pl.loop(0, rows // 2, unroll=2)
    def _(h):
        both = jnp.concatenate([pf[2 * h], pf[2 * h + 1]], axis=1)
        high, low = split(both)
        pt[h] = jnp.concatenate([high, low], axis=0).astype(BF16)

    lane = lax.broadcasted_iota(jnp.int32, (OB, lanes), 1)

    energies = jnp.zeros((OB, lanes), F32)
    for a in range(4):
        for m in range(4):
            energies = jnp.where(lane == 64 + 4 * a + m, kb_ref[a : a + 1, m : m + 1], energies)

    def project(stage, first, count):
        def step(h, acc):
            both = jnp.concatenate(
                [
                    jnp.concatenate(
                        [ext[stage, first + i, rows + 2 * h + j] for i in range(count)], axis=0
                    )
                    for j in range(2)
                ],
                axis=1,
            )
            high, low = split(both)
            left = jnp.concatenate([high, low], axis=0).astype(BF16)
            return acc + lax.dot_general(left, pt[h], NT, preferred_element_type=F32)

        most = count * OB
        acc = lax.fori_loop(0, rows // 2, step, jnp.zeros((2 * most, lanes), F32), unroll=4)
        total = acc[:most] + acc[most:] + pltpu.roll(acc[:most], 64, 1)
        for i in range(count):
            pay[stage, first + i] = jnp.where(
                lane < 48, total[i * OB : (i + 1) * OB], energies
            )
            for partner in range(4):
                partial_copy(stage, first + i, partner).start()

    project(0, 0, chunks)
    advance(2)

    def returned(stage, c):
        for i in range(4):
            partial_copy(stage, c, i).wait_recv()
        above2, above1, below1, below2 = (prec[stage, c, i] for i in range(4))
        own = pay[stage, c]
        total = (
            own
            + jnp.where(lane < 32, pltpu.roll(below1, 112, 1), 0.0)
            + jnp.where(lane >= 16, pltpu.roll(above1, 16, 1), 0.0)
            + jnp.where(lane < 16, pltpu.roll(below2, 96, 1), 0.0)
            + jnp.where(lane >= 32, pltpu.roll(above2, 32, 1), 0.0)
        )
        energy = jnp.where(
            lane < 16,
            pltpu.roll(below1, 64, 1),
            jnp.where(lane < 32, pltpu.roll(own, 80, 1), pltpu.roll(above1, 96, 1)),
        )
        total = jnp.where(lane < 48, total * energy, 0.0)
        high, low = split(total)
        return high + pltpu.roll(high, 64, 1), low

    def contribute(stage, first, count):
        parts = [returned(stage, first + i) for i in range(count)]
        coeff = jnp.concatenate(
            [high for high, _ in parts] + [low for _, low in parts], axis=0
        ).astype(BF16)
        most = count * OB

        @pl.loop(0, rows // 2, unroll=4)
        def _(h):
            part = jnp.dot(coeff, pt[h], preferred_element_type=F32)
            part = part[:most] + part[most:]
            for i in range(count):
                for half in range(2):
                    con[first + i, 2 * h + half] = part[
                        i * OB : (i + 1) * OB, half * lanes : (half + 1) * lanes
                    ]

    weight_y = [0.0] * ny
    for k in range(1, 7):
        weight_y[k % ny] += LAP_COEF[k]
        weight_y[-k % ny] += LAP_COEF[k]

    def hamilton(stage, c, scale, put):
        halo(stage, c, 0).wait_recv()
        halo(stage, c, 1).wait_recv()

        @pl.loop(0, planes)
        def _(z):
            base = rows + z * ny
            centre = [ext[stage, c, base + y] for y in range(ny)]
            v = v_ref[pl.ds(pl.multiple_of(z * ny, ny), ny), :]
            for y in range(ny):
                f = centre[y]
                acc = con[c, z * ny + y]
                own = v[y : y + 1, :] + (
                    -1.5 * LAP_COEF[0] - CENTRE - 0.5 * weight_y[0]
                )
                acc = acc + own * f
                for k in range(1, 7):
                    both = (
                        ext[stage, c, base + y + ny * k]
                        + ext[stage, c, base + y - ny * k]
                        + pltpu.roll(f, k, 1)
                        + pltpu.roll(f, lanes - k, 1)
                    )
                    acc = acc + (-0.5 * LAP_COEF[k]) * both
                for k in range(1, ny // 2):
                    acc = acc + (-0.5 * weight_y[k]) * (
                        centre[(y + k) % ny] + centre[(y - k) % ny]
                    )
                acc = acc + (-0.5 * weight_y[ny // 2]) * centre[(y + ny // 2) % ny]
                put(z * ny + y, scale * acc)

    contribute(0, 0, chunks)

    def first_stage(c):
        def put(r, value):
            ext[1, c, rows + r] = value

        hamilton(0, c, SIGMA / HALF_WIDTH, put)

    first_stage(0)
    advance(3)
    first_stage(1)
    project(1, 0, 2)
    advance(4)
    first_stage(2)
    first_stage(3)
    project(1, 2, 2)
    advance(5)
    contribute(1, 0, 2)

    def quarter_copy(c, d):
        other = orb_id(d)
        return pltpu.make_async_remote_copy(
            src_ref=fbuf.at[c, pl.ds(other * quarter, quarter)],
            dst_ref=abuf.at[n_orb - d, c],
            send_sem=a_send.at[c, d],
            recv_sem=a_recv.at[c, n_orb - d],
            device_id=(g, other),
            device_id_type=MESH,
        )

    def quarter_arrival(c, d):
        return pltpu.make_async_remote_copy(
            src_ref=fbuf.at[c, pl.ds(0, quarter)],
            dst_ref=abuf.at[d, c],
            send_sem=a_send.at[c, d],
            recv_sem=a_recv.at[c, d],
            device_id=(g, orb_id(d)),
            device_id_type=MESH,
        )

    def out_copy(c):
        part = pl.ds(c * OB * rows, OB * rows)
        return pltpu.make_async_copy(out_ref.at[part], out_hbm.at[part], out_sem.at[c])

    def second_stage(c):
        def put(r, value):
            value = value + (-SIGMA * SIGMA_TWO) * ext[0, c, rows + r]
            fbuf[c, r] = value
            out_ref[pl.ds(c * OB * rows + r, OB, stride=rows), :] = value

        hamilton(1, c, 2.0 * SIGMA_TWO / HALF_WIDTH, put)
        for d in range(1, n_orb):
            quarter_copy(c, d).start()
        out_copy(c).start()
        abuf[0, c] = fbuf[c, pl.ds(o * quarter, quarter)]

    second_stage(0)
    advance(6)
    second_stage(1)
    advance(7)
    contribute(1, 2, 2)
    second_stage(2)
    second_stage(3)

    for d in range(1, n_orb):
        @pl.loop(0, chunks)
        def _(c):
            quarter_arrival(c, d).wait_recv()

    per = chunks * OB
    norb = n_orb * per

    @pl.loop(0, n_orb)
    def _(b):
        slot = lax.rem(b - o + n_orb, n_orb)
        place = pl.multiple_of(b * per, per)
        for r in range(quarter):
            block = abuf[slot, :, r].reshape(per, lanes)
            high, low = split(block)
            ah[pl.ds(place, per), r * lanes : (r + 1) * lanes] = high.astype(BF16)
            ah[pl.ds(norb + place, per), r * lanes : (r + 1) * lanes] = low.astype(BF16)

    prod = lax.dot_general(ah[0:norb], ah[...], NT, preferred_element_type=F32)
    gbuf[...] = prod[:, :norb] + prod[:, norb:]
    prod = lax.dot_general(ah[norb:], ah[0:norb], NT, preferred_element_type=F32)
    gbuf[...] += prod

    def rows_copy(d):
        other = orb_id(d)
        return pltpu.make_async_remote_copy(
            src_ref=gbuf.at[pl.ds(pl.multiple_of(other * per, per), per)],
            dst_ref=grecv.at[n_orb - d],
            send_sem=g_send.at[d],
            recv_sem=g_recv.at[n_orb - d],
            device_id=(g, other),
            device_id_type=MESH,
        )

    def rows_arrival(d):
        return pltpu.make_async_remote_copy(
            src_ref=gbuf.at[pl.ds(0, per)],
            dst_ref=grecv.at[d],
            send_sem=g_send.at[d],
            recv_sem=g_recv.at[d],
            device_id=(g, orb_id(d)),
            device_id_type=MESH,
        )

    for d in range(1, n_orb):
        rows_copy(d).start()
    total = gbuf[pl.ds(pl.multiple_of(o * per, per), per)]
    for d in range(1, n_orb):
        rows_arrival(d).wait_recv()
        total = total + grecv[d]
    sbuf[...] = total

    def sum_copy(d):
        return pltpu.make_async_remote_copy(
            src_ref=sbuf,
            dst_ref=srecv.at[n_grid - d],
            send_sem=s_send.at[d],
            recv_sem=s_recv.at[n_grid - d],
            device_id=(grid_id(d), o),
            device_id_type=MESH,
        )

    def sum_arrival(d):
        return pltpu.make_async_remote_copy(
            src_ref=sbuf,
            dst_ref=srecv.at[d],
            send_sem=s_send.at[d],
            recv_sem=s_recv.at[d],
            device_id=(grid_id(d), o),
            device_id_type=MESH,
        )

    @pl.loop(1, n_grid)
    def _(d):
        sum_copy(d).start()

    @pl.loop(1, n_grid)
    def _(d):
        sum_arrival(d).wait_recv()

    total = sbuf[...]
    total = lax.fori_loop(1, n_grid, lambda d, acc: acc + srecv[d], total)
    columns = norb // n_grid
    total = pltpu.roll(total, lax.rem(norb - g * columns, norb), 1)
    gram_ref[...] = total.T[:columns] * (1.0 / (n_grid * rows * lanes))

    @pl.loop(0, chunks)
    def _(c):
        out_copy(c).wait()
        for stage in range(2):
            for i in range(4):
                partial_copy(stage, c, i).wait_send()
        for d in range(1, n_orb):
            quarter_copy(c, d).wait_send()

    halo_left(1, chunks - 1)

    for d in range(1, n_orb):
        rows_copy(d).wait_send()

    @pl.loop(1, n_grid)
    def _(d):
        sum_copy(d).wait_send()


def on_device(psi_in, v_local, proj_index, proj_value, kb_energy):
    n_grid = lax.axis_size("grid")
    n_orb = lax.axis_size("orb")
    orbitals, planes, ny, nx = psi_in.shape
    rows = planes * ny
    chunks = orbitals // OB
    norb = orbitals * n_orb
    quarter = rows // n_orb
    psi = psi_in.reshape(orbitals * rows, nx)
    v = v_local.reshape(rows, nx)
    index = proj_index.reshape(6, 1, 2 * nx)
    value = proj_value.reshape(6, 8, nx)
    dma = pltpu.SemaphoreType.DMA
    vmem = pl.BlockSpec(memory_space=pltpu.VMEM)
    hbm = pl.BlockSpec(memory_space=pltpu.HBM)
    filtered, gram = pl.pallas_call(
        functools.partial(kernel, n_grid, n_orb, ny, planes, chunks),
        out_shape=(
            jax.ShapeDtypeStruct((orbitals * rows, nx), F32),
            jax.ShapeDtypeStruct((norb // n_grid, orbitals), F32),
        ),
        in_specs=[hbm] * 5,
        out_specs=(hbm, vmem),
        scratch_shapes=[
            pltpu.VMEM(psi.shape, F32),
            pltpu.VMEM(psi.shape, F32),
            pltpu.VMEM(v.shape, F32),
            pltpu.VMEM(index.shape, jnp.int32),
            pltpu.VMEM(value.shape, F32),
            pltpu.VMEM(kb_energy.shape, F32),
            pltpu.VMEM((chunks, rows, OB, nx), F32),
            pltpu.VMEM((2, chunks, 3 * rows, OB, nx), F32),
            pltpu.VMEM((rows, KP, nx), F32),
            pltpu.VMEM((rows // 2, 2 * KP, 2 * nx), BF16),
            pltpu.VMEM((chunks, rows, OB, nx), F32),
            pltpu.VMEM((n_orb, chunks, quarter, OB, nx), F32),
            pltpu.VMEM((2 * norb, quarter * nx), BF16),
            pltpu.VMEM((norb, norb), F32),
            pltpu.VMEM((n_orb, orbitals, norb), F32),
            pltpu.VMEM((orbitals, norb), F32),
            pltpu.VMEM((n_grid, orbitals, norb), F32),
            pltpu.VMEM((2, chunks, OB, nx), F32),
            pltpu.VMEM((2, chunks, 4, OB, nx), F32),
            dma((2, chunks, 2)),
            dma((2, chunks, 2)),
            dma((2, chunks, 4)),
            dma((2, chunks, 4)),
            dma((chunks, n_orb)),
            dma((chunks, n_orb)),
            dma((n_orb,)),
            dma((n_orb,)),
            dma((n_grid,)),
            dma((n_grid,)),
            dma((4,)),
            dma((chunks,)),
            dma((chunks,)),
        ],
        compiler_params=pltpu.CompilerParams(
            collective_id=0, has_side_effects=True, vmem_limit_bytes=62 * 1024 * 1024
        ),
        cost_estimate=pl.CostEstimate(
            flops=400_000_000, bytes_accessed=2_000_000, transcendentals=0
        ),
    )(psi, v, index, value, kb_energy)
    return filtered.reshape(psi_in.shape), gram.T


def solution(mesh):
    placed = (
        P("orb", "grid", None, None),
        P("grid", None, None),
        P("grid", None, None),
        P("grid", None, None, None),
        P("grid", None),
    )
    return jax.shard_map(
        on_device,
        mesh=mesh,
        in_specs=placed,
        out_specs=(P("orb", "grid", None, None), P("orb", "grid")),
        check_vma=False,
    )
```

```python
import functools

import jax
import jax.numpy as jnp
from jax import lax
from jax.experimental import pallas as pl
from jax.experimental.pallas import tpu as pltpu
from jax.sharding import PartitionSpec as P

LAP_COEF = (
    -5369.0 / 1800.0,
    12.0 / 7.0,
    -15.0 / 56.0,
    10.0 / 189.0,
    -1.0 / 112.0,
    2.0 / 1925.0,
    -1.0 / 16632.0,
)
HALF_WIDTH = 6.0
CENTRE = 8.0
SIGMA = HALF_WIDTH / (-3.0 - CENTRE)
SIGMA_TWO = 1.0 / (2.0 / SIGMA - SIGMA)
MESH = pl.DeviceIdType.MESH
OB = 8
KP = 64
PAIR_PARTNERS = (-2, -1, 1, 2)
F32 = jnp.float32
BF16 = jnp.bfloat16
NT = (((1,), (1,)), ((), ()))


def split(x):
    high = x.astype(BF16).astype(F32)
    return high, x - high


def kernel(
    n_grid, n_orb, ny, planes, chunks,
    psi_hbm, v_hbm, idx_hbm, val_hbm, kb_hbm,
    out_hbm, gram_ref,
    out_ref,    psi_ref, v_ref, idx_ref, val_ref, kb_ref, con, ext, pf, pt, fbuf, abuf, ah, gbuf, grecv, sbuf, srecv, pay, prec,
    h_send, h_recv, p_send, p_recv, a_send, a_recv, g_send, g_recv, s_send, s_recv, in_sem, psi_sem, out_sem,
):
    rows = ny * planes
    quarter = rows // n_orb
    lanes = 128
    g = lax.axis_index("grid")
    o = lax.axis_index("orb")

    def grid_id(d):
        return lax.rem(g + d + n_grid, n_grid)

    def orb_id(d):
        return lax.rem(o + d, n_orb)

    def psi_copy(c):
        part = pl.ds(c * OB * rows, OB * rows)
        return pltpu.make_async_copy(psi_hbm.at[part], psi_ref.at[part], psi_sem.at[c])

    small = [
        pltpu.make_async_copy(src, dst, in_sem.at[i])
        for i, (src, dst) in enumerate(
            ((idx_hbm, idx_ref), (val_hbm, val_ref), (kb_hbm, kb_ref), (v_hbm, v_ref))
        )
    ]

    @pl.loop(0, chunks)
    def _(c):
        psi_copy(c).start()

    for copy in small:
        copy.start()

    barrier = pltpu.get_barrier_semaphore()

    @pl.loop(1, n_grid)
    def _(d):
        pl.semaphore_signal(barrier, inc=1, device_id=(grid_id(d), o), device_id_type=MESH)

    for d in range(1, n_orb):
        pl.semaphore_signal(barrier, inc=1, device_id=(g, orb_id(d)), device_id_type=MESH)

    def stage_in(c):
        psi_copy(c).wait()

        @pl.loop(0, rows, unroll=8)
        def _(r):
            ext[0, c, rows + r] = psi_ref[pl.ds(c * OB * rows + r, OB, stride=rows), :]

    stage_in(0)
    pl.semaphore_wait(barrier, n_grid - 1 + n_orb - 1)

    def halo(stage, c, side):
        return pltpu.make_async_remote_copy(
            src_ref=ext.at[stage, c, pl.ds(rows, rows)],
            dst_ref=ext.at[stage, c, pl.ds(0 if side == 0 else 2 * rows, rows)],
            send_sem=h_send.at[stage, c, side],
            recv_sem=h_recv.at[stage, c, side],
            device_id=(grid_id(1 if side == 0 else -1), o),
            device_id_type=MESH,
        )

    def partial_copy(stage, c, i):
        return pltpu.make_async_remote_copy(
            src_ref=pay.at[stage, c],
            dst_ref=prec.at[stage, c, i],
            send_sem=p_send.at[stage, c, i],
            recv_sem=p_recv.at[stage, c, i],
            device_id=(grid_id(PAIR_PARTNERS[i]), o),
            device_id_type=MESH,
        )

    def halo_start(stage, c):
        halo(stage, c, 0).start()
        halo(stage, c, 1).start()

    def halo_left(stage, c):
        halo(stage, c, 0).wait_send()
        halo(stage, c, 1).wait_send()

    def advance(k):
        halo_left((k - 1) // chunks, (k - 1) % chunks)
        halo_start(k // chunks, k % chunks)

    halo_start(0, 0)
    pl.loop(1, chunks)(stage_in)
    for copy in small:
        copy.wait()

    pf[:, 48:KP, :] = jnp.zeros((rows, KP - 48, lanes), F32)

    @pl.loop(0, 6)
    def _(q):
        value = val_ref[q]
        upper = lax.broadcasted_iota(jnp.int32, (8, lanes), 0) < 4
        value = jnp.concatenate(
            [jnp.where(upper, value, 0.0), jnp.where(upper, 0.0, value)], axis=1
        )
        index = idx_ref[q]
        high = jnp.broadcast_to(index >> 7, (8, 2 * lanes))
        low = jnp.broadcast_to(index & 127, (lanes, 2 * lanes))
        hot = jnp.where(
            lax.broadcasted_iota(jnp.int32, (lanes, 2 * lanes), 0) == low, 1.0, 0.0
        ).astype(BF16)
        vh, vl = split(value)
        left = jnp.concatenate(
            [jnp.where(high == h, vh, 0.0) for h in range(rows)], axis=0
        ).astype(BF16)
        dense = lax.dot_general(left, hot, NT, preferred_element_type=F32)
        left = jnp.concatenate(
            [jnp.where(high == h, vl, 0.0) for h in range(rows)], axis=0
        ).astype(BF16)
        dense = dense + lax.dot_general(left, hot, NT, preferred_element_type=F32)
        pf[:, pl.ds(pl.multiple_of(q * 8, 8), 8), :] = dense.reshape(rows, 8, lanes)

    advance(1)

    @pl.loop(0, rows // 2, unroll=2)
    def _(h):
        both = jnp.concatenate([pf[2 * h], pf[2 * h + 1]], axis=1)
        high, low = split(both)
        pt[h] = jnp.concatenate([high, low], axis=0).astype(BF16)

    lane = lax.broadcasted_iota(jnp.int32, (OB, lanes), 1)

    energies = jnp.zeros((OB, lanes), F32)
    for a in range(4):
        for m in range(4):
            energies = jnp.where(lane == 64 + 4 * a + m, kb_ref[a : a + 1, m : m + 1], energies)

    def project(stage, first, count):
        def step(h, acc):
            both = jnp.concatenate(
                [
                    jnp.concatenate(
                        [ext[stage, first + i, rows + 2 * h + j] for i in range(count)], axis=0
                    )
                    for j in range(2)
                ],
                axis=1,
            )
            high, low = split(both)
            left = jnp.concatenate([high, low], axis=0).astype(BF16)
            return acc + lax.dot_general(left, pt[h], NT, preferred_element_type=F32)

        most = count * OB
        acc = lax.fori_loop(0, rows // 2, step, jnp.zeros((2 * most, lanes), F32), unroll=4)
        total = acc[:most] + acc[most:] + pltpu.roll(acc[:most], 64, 1)
        for i in range(count):
            pay[stage, first + i] = jnp.where(
                lane < 48, total[i * OB : (i + 1) * OB], energies
            )
            for partner in range(4):
                partial_copy(stage, first + i, partner).start()

    project(0, 0, chunks)
    advance(2)

    def returned(stage, c):
        for i in range(4):
            partial_copy(stage, c, i).wait_recv()
        above2, above1, below1, below2 = (prec[stage, c, i] for i in range(4))
        own = pay[stage, c]
        total = (
            own
            + jnp.where(lane < 32, pltpu.roll(below1, 112, 1), 0.0)
            + jnp.where(lane >= 16, pltpu.roll(above1, 16, 1), 0.0)
            + jnp.where(lane < 16, pltpu.roll(below2, 96, 1), 0.0)
            + jnp.where(lane >= 32, pltpu.roll(above2, 32, 1), 0.0)
        )
        energy = jnp.where(
            lane < 16,
            pltpu.roll(below1, 64, 1),
            jnp.where(lane < 32, pltpu.roll(own, 80, 1), pltpu.roll(above1, 96, 1)),
        )
        total = jnp.where(lane < 48, total * energy, 0.0)
        high, low = split(total)
        return high + pltpu.roll(high, 64, 1), low

    def contribute(stage, first, count):
        parts = [returned(stage, first + i) for i in range(count)]
        coeff = jnp.concatenate(
            [high for high, _ in parts] + [low for _, low in parts], axis=0
        ).astype(BF16)
        most = count * OB

        @pl.loop(0, rows // 2, unroll=4)
        def _(h):
            part = jnp.dot(coeff, pt[h], preferred_element_type=F32)
            part = part[:most] + part[most:]
            for i in range(count):
                for half in range(2):
                    con[first + i, 2 * h + half] = part[
                        i * OB : (i + 1) * OB, half * lanes : (half + 1) * lanes
                    ]

    weight_y = [0.0] * ny
    for k in range(1, 7):
        weight_y[k % ny] += LAP_COEF[k]
        weight_y[-k % ny] += LAP_COEF[k]

    def hamilton(stage, c, scale, put):
        halo(stage, c, 0).wait_recv()
        halo(stage, c, 1).wait_recv()

        @pl.loop(0, planes)
        def _(z):
            base = rows + z * ny
            centre = [ext[stage, c, base + y] for y in range(ny)]
            v = v_ref[pl.ds(pl.multiple_of(z * ny, ny), ny), :]
            for y in range(ny):
                f = centre[y]
                acc = con[c, z * ny + y]
                own = v[y : y + 1, :] + (
                    -1.5 * LAP_COEF[0] - CENTRE - 0.5 * weight_y[0]
                )
                acc = acc + own * f
                for k in range(1, 7):
                    both = (
                        ext[stage, c, base + y + ny * k]
                        + ext[stage, c, base + y - ny * k]
                        + pltpu.roll(f, k, 1)
                        + pltpu.roll(f, lanes - k, 1)
                    )
                    acc = acc + (-0.5 * LAP_COEF[k]) * both
                for k in range(1, ny // 2):
                    acc = acc + (-0.5 * weight_y[k]) * (
                        centre[(y + k) % ny] + centre[(y - k) % ny]
                    )
                acc = acc + (-0.5 * weight_y[ny // 2]) * centre[(y + ny // 2) % ny]
                put(z * ny + y, scale * acc)

    contribute(0, 0, chunks)

    def first_stage(c):
        def put(r, value):
            ext[1, c, rows + r] = value

        hamilton(0, c, SIGMA / HALF_WIDTH, put)

    first_stage(0)
    advance(3)
    first_stage(1)
    project(1, 0, 2)
    advance(4)
    first_stage(2)
    first_stage(3)
    project(1, 2, 2)
    advance(5)
    contribute(1, 0, 2)

    def quarter_copy(c, d):
        other = orb_id(d)
        return pltpu.make_async_remote_copy(
            src_ref=fbuf.at[c, pl.ds(other * quarter, quarter)],
            dst_ref=abuf.at[n_orb - d, c],
            send_sem=a_send.at[c, d],
            recv_sem=a_recv.at[c, n_orb - d],
            device_id=(g, other),
            device_id_type=MESH,
        )

    def quarter_arrival(c, d):
        return pltpu.make_async_remote_copy(
            src_ref=fbuf.at[c, pl.ds(0, quarter)],
            dst_ref=abuf.at[d, c],
            send_sem=a_send.at[c, d],
            recv_sem=a_recv.at[c, d],
            device_id=(g, orb_id(d)),
            device_id_type=MESH,
        )

    def out_copy(c):
        part = pl.ds(c * OB * rows, OB * rows)
        return pltpu.make_async_copy(out_ref.at[part], out_hbm.at[part], out_sem.at[c])

    def second_stage(c):
        def put(r, value):
            value = value + (-SIGMA * SIGMA_TWO) * ext[0, c, rows + r]
            fbuf[c, r] = value
            out_ref[pl.ds(c * OB * rows + r, OB, stride=rows), :] = value

        hamilton(1, c, 2.0 * SIGMA_TWO / HALF_WIDTH, put)
        for d in range(1, n_orb):
            quarter_copy(c, d).start()
        out_copy(c).start()
        abuf[0, c] = fbuf[c, pl.ds(o * quarter, quarter)]

    second_stage(0)
    advance(6)
    second_stage(1)
    advance(7)
    contribute(1, 2, 2)
    second_stage(2)
    second_stage(3)

    for d in range(1, n_orb):
        @pl.loop(0, chunks)
        def _(c):
            quarter_arrival(c, d).wait_recv()

    per = chunks * OB
    norb = n_orb * per

    @pl.loop(0, n_orb)
    def _(b):
        slot = lax.rem(b - o + n_orb, n_orb)
        place = pl.multiple_of(b * per, per)
        for r in range(quarter):
            block = abuf[slot, :, r].reshape(per, lanes)
            high, low = split(block)
            ah[pl.ds(place, per), r * lanes : (r + 1) * lanes] = high.astype(BF16)
            ah[pl.ds(norb + place, per), r * lanes : (r + 1) * lanes] = low.astype(BF16)

    prod = lax.dot_general(ah[...], ah[0:norb], NT, preferred_element_type=F32)
    gbuf[...] = prod[:norb] + prod[norb:] + prod[norb:].T

    def rows_copy(d):
        other = orb_id(d)
        return pltpu.make_async_remote_copy(
            src_ref=gbuf.at[pl.ds(pl.multiple_of(other * per, per), per)],
            dst_ref=grecv.at[n_orb - d],
            send_sem=g_send.at[d],
            recv_sem=g_recv.at[n_orb - d],
            device_id=(g, other),
            device_id_type=MESH,
        )

    def rows_arrival(d):
        return pltpu.make_async_remote_copy(
            src_ref=gbuf.at[pl.ds(0, per)],
            dst_ref=grecv.at[d],
            send_sem=g_send.at[d],
            recv_sem=g_recv.at[d],
            device_id=(g, orb_id(d)),
            device_id_type=MESH,
        )

    for d in range(1, n_orb):
        rows_copy(d).start()
    total = gbuf[pl.ds(pl.multiple_of(o * per, per), per)]
    for d in range(1, n_orb):
        rows_arrival(d).wait_recv()
        total = total + grecv[d]
    sbuf[...] = total

    def sum_copy(d):
        return pltpu.make_async_remote_copy(
            src_ref=sbuf,
            dst_ref=srecv.at[n_grid - d],
            send_sem=s_send.at[d],
            recv_sem=s_recv.at[n_grid - d],
            device_id=(grid_id(d), o),
            device_id_type=MESH,
        )

    def sum_arrival(d):
        return pltpu.make_async_remote_copy(
            src_ref=sbuf,
            dst_ref=srecv.at[d],
            send_sem=s_send.at[d],
            recv_sem=s_recv.at[d],
            device_id=(grid_id(d), o),
            device_id_type=MESH,
        )

    @pl.loop(1, n_grid)
    def _(d):
        sum_copy(d).start()

    @pl.loop(1, n_grid)
    def _(d):
        sum_arrival(d).wait_recv()

    total = sbuf[...]
    total = lax.fori_loop(1, n_grid, lambda d, acc: acc + srecv[d], total)
    columns = norb // n_grid
    total = pltpu.roll(total, lax.rem(norb - g * columns, norb), 1)
    gram_ref[...] = total.T[:columns] * (1.0 / (n_grid * rows * lanes))

    @pl.loop(0, chunks)
    def _(c):
        out_copy(c).wait()
        for stage in range(2):
            for i in range(4):
                partial_copy(stage, c, i).wait_send()
        for d in range(1, n_orb):
            quarter_copy(c, d).wait_send()

    halo_left(1, chunks - 1)

    for d in range(1, n_orb):
        rows_copy(d).wait_send()

    @pl.loop(1, n_grid)
    def _(d):
        sum_copy(d).wait_send()


def on_device(psi_in, v_local, proj_index, proj_value, kb_energy):
    n_grid = lax.axis_size("grid")
    n_orb = lax.axis_size("orb")
    orbitals, planes, ny, nx = psi_in.shape
    rows = planes * ny
    chunks = orbitals // OB
    norb = orbitals * n_orb
    quarter = rows // n_orb
    psi = psi_in.reshape(orbitals * rows, nx)
    v = v_local.reshape(rows, nx)
    index = proj_index.reshape(6, 1, 2 * nx)
    value = proj_value.reshape(6, 8, nx)
    dma = pltpu.SemaphoreType.DMA
    vmem = pl.BlockSpec(memory_space=pltpu.VMEM)
    hbm = pl.BlockSpec(memory_space=pltpu.HBM)
    filtered, gram = pl.pallas_call(
        functools.partial(kernel, n_grid, n_orb, ny, planes, chunks),
        out_shape=(
            jax.ShapeDtypeStruct((orbitals * rows, nx), F32),
            jax.ShapeDtypeStruct((norb // n_grid, orbitals), F32),
        ),
        in_specs=[hbm] * 5,
        out_specs=(hbm, vmem),
        scratch_shapes=[
            pltpu.VMEM(psi.shape, F32),
            pltpu.VMEM(psi.shape, F32),
            pltpu.VMEM(v.shape, F32),
            pltpu.VMEM(index.shape, jnp.int32),
            pltpu.VMEM(value.shape, F32),
            pltpu.VMEM(kb_energy.shape, F32),
            pltpu.VMEM((chunks, rows, OB, nx), F32),
            pltpu.VMEM((2, chunks, 3 * rows, OB, nx), F32),
            pltpu.VMEM((rows, KP, nx), F32),
            pltpu.VMEM((rows // 2, 2 * KP, 2 * nx), BF16),
            pltpu.VMEM((chunks, rows, OB, nx), F32),
            pltpu.VMEM((n_orb, chunks, quarter, OB, nx), F32),
            pltpu.VMEM((2 * norb, quarter * nx), BF16),
            pltpu.VMEM((norb, norb), F32),
            pltpu.VMEM((n_orb, orbitals, norb), F32),
            pltpu.VMEM((orbitals, norb), F32),
            pltpu.VMEM((n_grid, orbitals, norb), F32),
            pltpu.VMEM((2, chunks, OB, nx), F32),
            pltpu.VMEM((2, chunks, 4, OB, nx), F32),
            dma((2, chunks, 2)),
            dma((2, chunks, 2)),
            dma((2, chunks, 4)),
            dma((2, chunks, 4)),
            dma((chunks, n_orb)),
            dma((chunks, n_orb)),
            dma((n_orb,)),
            dma((n_orb,)),
            dma((n_grid,)),
            dma((n_grid,)),
            dma((4,)),
            dma((chunks,)),
            dma((chunks,)),
        ],
        compiler_params=pltpu.CompilerParams(
            collective_id=0, has_side_effects=True, vmem_limit_bytes=62 * 1024 * 1024
        ),
        cost_estimate=pl.CostEstimate(
            flops=400_000_000, bytes_accessed=2_000_000, transcendentals=0
        ),
    )(psi, v, index, value, kb_energy)
    return filtered.reshape(psi_in.shape), gram.T


def solution(mesh):
    placed = (
        P("orb", "grid", None, None),
        P("grid", None, None),
        P("grid", None, None),
        P("grid", None, None, None),
        P("grid", None),
    )
    return jax.shard_map(
        on_device,
        mesh=mesh,
        in_specs=placed,
        out_specs=(P("orb", "grid", None, None), P("orb", "grid")),
        check_vma=False,
    )
```
